32 devices in a mesh: dp: 4 (over x, core), hidden: 8 (over z, y).
Axes of the slice: x: 2, y: 2, z: 4, core: 2. Of those that a mesh axis runs over, the one named last changes fastest.
Arguments:
- features: bfloat16 [32768, 16384], P('dp', 'hidden'), may hold values from -0.046875 to 0.046875
- codes: int32 [32768], P('dp'), may hold values from 1 to 8
- targets: float32 [16384, 32], P('hidden'), may hold values from -6 to 6
- guess: float32 [16384, 32], P('hidden'), may hold values from -4 to 4
Outputs:
- solution: float32 [16384, 32], P('hidden')
- residual: float32 [16384, 32], P('hidden')
The draws below stay inside these ranges and needn't reach their ends.
All inputs are finite; a program needn't handle non-finite values.
Results may differ from the reference program's by a relative error of at most 0.011.
Values may be sent and summed in bfloat16 or wider, within the bound.
A program may use at most 128 MiB of HBM per device.

```python
import jax
import jax.numpy as jnp
from jax import lax

WIDTH = 16384
RHS = 32
ITERS = 2
ROWS = 32768


def place_ends(values, key, smallest, high):
    dims = values.shape
    index_at = [jax.random.randint(jax.random.fold_in(key, axis), (), 0, dims[axis]) for axis in range(len(dims))]
    values = values.at[tuple(index_at)].set(smallest)
    longest = dims.index(max(dims))
    index_at[longest] = (index_at[longest] + 1) % dims[longest]
    return values.at[tuple(index_at)].set(high)


def block_scale(stream_key, dims, split, smallest, largest):
    loudness, own = 1.0, jax.random.fold_in(stream_key, 6)
    for axis_at, parts in split:
        steps = jnp.exp(jax.random.uniform(jax.random.fold_in(own, axis_at), (parts,), jnp.float32, smallest / len(split), largest / len(split)))
        loudness = loudness * jnp.repeat(steps, dims[axis_at] // parts).reshape([-1 if axis == axis_at else 1 for axis in range(len(dims))])
    return loudness


def normal_values(rng, shape, spread, most, split=(), held_as=jnp.bfloat16):
    array = spread * jax.random.normal(rng, shape, jnp.float32)
    if split:
        array = array * block_scale(rng, shape, split, -0.22, 0.18)
    return jnp.clip(array, -most, most).astype(held_as)


def setup_inputs(seed: int = 0) -> dict:
    arg_keys = jax.random.split(jax.random.key(seed), 5)
    features = normal_values(arg_keys[0], (ROWS, WIDTH), WIDTH ** -0.5, 0.046875, ((0, 4), (1, 8)))
    codes = place_ends(jax.random.randint(arg_keys[1], (ROWS,), 1, 9), jax.random.fold_in(arg_keys[1], 1), 1, 8).astype(jnp.int32)
    targets = normal_values(arg_keys[2], (WIDTH, RHS), 1.0, 6.0, ((0, 8),), jnp.float32)
    guess = normal_values(arg_keys[3], (WIDTH, RHS), 0.3, 4.0, ((0, 8),), jnp.float32)
    return {"features": features, "codes": codes, "targets": targets, "guess": guess}


damping = 0.5
code_scale = 0.25

def apply_operator(features, weights, vectors):
    rounded = vectors.astype(jnp.bfloat16)
    rowprod = jnp.dot(features.astype(jnp.float32), rounded.astype(jnp.float32), preferred_element_type=jnp.float32)
    scaled = (weights[:, None] * rowprod).astype(jnp.bfloat16)
    back = lax.dot_general(features.astype(jnp.float32), scaled.astype(jnp.float32), (((0,), (0,)), ((), ())), preferred_element_type=jnp.float32)
    return back + damping * vectors

def gram(left, right):
    return jnp.dot(left.T, right, precision=lax.Precision.HIGHEST)

def solve_small(matrix, rhs_block):
    factor = jnp.linalg.cholesky(0.5 * (matrix + matrix.T))
    middle = lax.linalg.triangular_solve(factor, rhs_block, left_side=True, lower=True)
    return lax.linalg.triangular_solve(factor, middle, left_side=True, lower=True, transpose_a=True)

def reference(features, codes, targets, guess):
    weights = codes.astype(jnp.float32) * code_scale
    solution = guess
    residual = targets - apply_operator(features, weights, guess)
    direction = residual
    norm_now = gram(residual, residual)
    for step in range(ITERS):
        applied = apply_operator(features, weights, direction)
        step_mix = solve_small(gram(direction, applied), norm_now)
        solution = solution + jnp.dot(direction, step_mix, precision=lax.Precision.HIGHEST)
        residual = residual - jnp.dot(applied, step_mix, precision=lax.Precision.HIGHEST)
        if step + 1 < ITERS:
            fresh = gram(residual, residual)
            mixing = solve_small(norm_now, fresh)
            direction = residual + jnp.dot(direction, mixing, precision=lax.Precision.HIGHEST)
            norm_now = fresh
    return (solution, residual)
```

```python
import functools

import jax
import jax.numpy as jnp
from jax import lax
from jax.experimental import pallas as pl
from jax.experimental.pallas import tpu as pltpu
from jax.sharding import PartitionSpec as P

ITERS = 2
damping = 0.5
code_scale = 0.25

F32 = jnp.float32
BF16 = jnp.bfloat16
NT = (((1,), (1,)), ((), ()))
TN = (((0,), (0,)), ((), ()))


def exact(a, b, dims):
    return lax.dot_general(a, b, dims, precision=lax.Precision.HIGHEST, preferred_element_type=F32)


def solve_small(matrix, rhs):
    left = 0.5 * (matrix + matrix.T)
    right = rhs
    size = left.shape[0]
    row_at = lax.broadcasted_iota(jnp.int32, left.shape, 0)
    for k in range(size):
        here = row_at == k
        inv = 1.0 / left[k : k + 1, k : k + 1]
        lrow = left[k : k + 1, :] * inv
        rrow = right[k : k + 1, :] * inv
        col = left[:, k : k + 1]
        left = jnp.where(here, lrow, left - col * lrow)
        right = jnp.where(here, rrow, right - col * rrow)
    return right


def kernel(nh, nd, f_hbm, codes_ref, t_ref, g_ref, sol_ref, res_ref,
           fv, rs_send, rs_recv, own, rows0, gr_send, gr_recv, ag, pg_send, pg_recv,
           acc, dr_recv, dg_send, dg_recv, dq, d_ref,
           f_sem, rs_ss, rs_rs, gr_ss, gr_rs, ag_ss, ag_rs, pg_ss, pg_rs,
           dr_ss, dr_rs, dg_ss, dg_rs, dq_ss, dq_rs):
    me = lax.axis_index("hidden")
    md = lax.axis_index("dp")
    tokens, width = fv.shape
    seg = tokens // nh
    part = width // nd

    def at_step(i):
        return ((i + nh // 2 - 1) % (nh - 1) + 1) * (1 - i // (nh - 1))

    def rows_of(index):
        return pl.ds(pl.multiple_of(index * seg, seg), seg)

    def f_copy(i):
        t = rows_of((me + at_step(i)) % nh)
        return pltpu.make_async_copy(f_hbm.at[t], fv.at[t], f_sem.at[i])

    def to_hidden(src, dst, ss, rs, d):
        return pltpu.make_async_remote_copy(
            src_ref=src, dst_ref=dst, send_sem=ss.at[d], recv_sem=rs.at[d],
            device_id={"hidden": (me + d) % nh}, device_id_type=pl.DeviceIdType.MESH)

    def to_dp(src, dst, ss, rs, e):
        return pltpu.make_async_remote_copy(
            src_ref=src, dst_ref=dst, send_sem=ss.at[e], recv_sem=rs.at[e],
            device_id={"dp": (md + e) % nd}, device_id_type=pl.DeviceIdType.MESH)

    rs_copy = lambda d: to_hidden(rs_send.at[d], rs_recv.at[d], rs_ss, rs_rs, d)
    gr_copy = lambda d: to_hidden(gr_send, gr_recv.at[d], gr_ss, gr_rs, d)
    ag_copy = lambda d: to_hidden(ag.at[0], ag.at[d], ag_ss, ag_rs, d)
    pg_copy = lambda d: to_hidden(pg_send, pg_recv.at[d], pg_ss, pg_rs, d)
    dr_copy = lambda e: to_dp(acc.at[(md + e) % nd], dr_recv.at[e], dr_ss, dr_rs, e)
    dg_copy = lambda k, e: to_dp(dg_send, dg_recv.at[k - 1, e], dg_ss.at[k - 1], dg_rs.at[k - 1], e)
    dq_send = lambda e: to_dp(dq.at[md], dq.at[md], dq_ss, dq_rs, e)
    dq_got = lambda e: to_dp(dq.at[md], dq.at[(md + nd - e) % nd], dq_ss, dq_rs, e)

    def each(start, stop, fn):
        def body(i, _):
            fn(i)
            return 0
        lax.fori_loop(start, stop, body, 0)

    each(0, nh, lambda i: f_copy(i).start())

    barrier = pltpu.get_barrier_semaphore()
    each(1, nh, lambda d: pl.semaphore_signal(
        barrier, inc=1, device_id={"hidden": (me + d) % nh}, device_id_type=pl.DeviceIdType.MESH))
    each(1, nd, lambda e: pl.semaphore_signal(
        barrier, inc=1, device_id={"dp": (md + e) % nd}, device_id_type=pl.DeviceIdType.MESH))
    pl.semaphore_wait(barrier, nh - 1 + nd - 1)

    weights = codes_ref[me].astype(F32) * code_scale

    norms = None
    for k in range(ITERS + 1):
        source = g_ref if k == 0 else res_ref
        vec = source[...].astype(BF16)
        if k > 0:
            gr_send[...] = exact(source[...], source[...], NT)
            each(1, nh, lambda d: gr_copy(d).start())

        def forward(i):
            d = at_step(i)
            if k == 0:
                f_copy(i).wait()
            r = lax.dot_general(vec, fv[rows_of((me + d) % nh), :], NT, preferred_element_type=F32)
            own[...] = r
            rs_send[d] = r.astype(BF16)

            @pl.when(i < nh - 1)
            def _():
                rs_copy(d).start()

        each(0, nh, forward)

        if k > 0:
            each(1, nh, lambda d: gr_copy(d).wait())
            fresh = gr_send[...]
            for d in range(1, nh):
                fresh = fresh + gr_recv[d]
            if k > 1:
                mix = solve_small(norms, fresh)
                d_ref[...] = res_ref[...] + exact(mix, d_ref[...], TN)
            norms = fresh

        each(1, nh, lambda i: rs_copy(i).wait())
        rows = own[...]
        for d in range(1, nh):
            rows = rows + rs_recv[d].astype(F32)
        if k > 1:
            rows = rows + exact(mix, rows0[...], TN)
        if 0 < k < ITERS:
            rows0[...] = rows
        scaled = (rows * weights).astype(BF16)
        ag[0] = scaled
        each(0, nh - 1, lambda i: ag_copy(at_step(i)).start())
        if k > 0:
            local = gr_send[...] if k == 1 else exact(d_ref[...], d_ref[...], NT)
            pg_send[...] = exact(rows, scaled.astype(F32), NT) + (damping / nd) * local
            each(1, nh, lambda d: pg_copy(d).start())

        def add_back(d, first):
            seg_rows = rows_of((me + nh - d) % nh)
            piece = ag[d]
            for c in range(nd):
                got = jnp.dot(piece, fv[seg_rows, c * part : (c + 1) * part], preferred_element_type=F32)
                acc[c] = got if first else acc[c] + got

        add_back(0, True)

        def backward(i):
            d = at_step(i)
            ag_copy(d).wait()
            add_back(d, False)

        each(0, nh - 1, backward)
        each(1, nd, lambda e: dr_copy(e).start())
        if k > 0:
            each(1, nh, lambda d: pg_copy(d).wait())
            dg = pg_send[...]
            for d in range(1, nh):
                dg = dg + pg_recv[d]
            dg_send[...] = dg
            each(1, nd, lambda e: dg_copy(k, e).start())
        each(1, nd, lambda e: dr_copy(e).wait())
        total = acc[md]
        for e in range(1, nd):
            total = total + dr_recv[e]
        dq[md] = total
        each(1, nd, lambda e: dq_send(e).start())
        if k > 0:
            each(1, nd, lambda e: dg_copy(k, e).wait())
            curv = dg_send[...]
            for e in range(1, nd):
                curv = curv + dg_recv[k - 1, e]
            step_mix = solve_small(curv, norms)
        each(1, nd, lambda e: dq_got(e).wait())
        applied = jnp.concatenate([dq[c] for c in range(nd)], axis=1)
        if k == 0:
            residual = t_ref[...] - (applied + damping * g_ref[...])
            res_ref[...] = residual
            d_ref[...] = residual
        else:
            applied = applied + damping * d_ref[...]
            before = g_ref[...] if k == 1 else sol_ref[...]
            sol_ref[...] = before + exact(step_mix, d_ref[...], TN)
            res_ref[...] = res_ref[...] - exact(step_mix, applied, TN)


def shards(nh, nd, features, codes, targets, guess):
    tokens, width = features.shape
    rhs = guess.shape[1]
    seg = tokens // nh
    part = width // nd
    vmem = pl.BlockSpec(memory_space=pltpu.VMEM)
    flat = jax.ShapeDtypeStruct((rhs, width), F32)
    dma = pltpu.SemaphoreType.DMA
    sol, res = pl.pallas_call(
        functools.partial(kernel, nh, nd),
        out_shape=(flat, flat),
        in_specs=[pl.BlockSpec(memory_space=pl.ANY), vmem, vmem, vmem],
        out_specs=(vmem, vmem),
        scratch_shapes=[
            pltpu.VMEM((tokens, width), BF16),
            pltpu.VMEM((nh, rhs, seg), BF16),
            pltpu.VMEM((nh, rhs, seg), BF16),
            pltpu.VMEM((rhs, seg), F32),
            pltpu.VMEM((rhs, seg), F32),
            pltpu.VMEM((rhs, rhs), F32),
            pltpu.VMEM((nh, rhs, rhs), F32),
            pltpu.VMEM((nh, rhs, seg), BF16),
            pltpu.VMEM((rhs, rhs), F32),
            pltpu.VMEM((nh, rhs, rhs), F32),
            pltpu.VMEM((nd, rhs, part), F32),
            pltpu.VMEM((nd, rhs, part), F32),
            pltpu.VMEM((rhs, rhs), F32),
            pltpu.VMEM((ITERS, nd, rhs, rhs), F32),
            pltpu.VMEM((nd, rhs, part), F32),
            pltpu.VMEM((rhs, width), F32),
            dma((nh,)),
            dma((nh,)), dma((nh,)), dma((nh,)), dma((nh,)),
            dma((nh,)), dma((nh,)), dma((nh,)), dma((nh,)),
            dma((nd,)), dma((nd,)), dma((ITERS, nd)), dma((ITERS, nd)), dma((nd,)), dma((nd,)),
        ],
        compiler_params=pltpu.CompilerParams(
            collective_id=0, has_side_effects=True, vmem_limit_bytes=56 * 1024 * 1024),
        cost_estimate=pl.CostEstimate(
            flops=12 * tokens * width * rhs, bytes_accessed=2 * tokens * width, transcendentals=0),
    )(features, codes.reshape(nh, 1, seg), targets.T, guess.T)
    return sol.T, res.T


def solution(mesh):
    nh, nd = mesh.shape["hidden"], mesh.shape["dp"]
    in_specs = (P("dp", "hidden"), P("dp"), P("hidden", None), P("hidden", None))
    out_specs = (P("hidden", None), P("hidden", None))
    return jax.shard_map(functools.partial(shards, nh, nd), mesh=mesh, in_specs=in_specs,
                         out_specs=out_specs, check_vma=False)
```

```python
import functools

import jax
import jax.numpy as jnp
from jax import lax
from jax.experimental import pallas as pl
from jax.experimental.pallas import tpu as pltpu
from jax.sharding import PartitionSpec as P

ITERS = 2
damping = 0.5
code_scale = 0.25

F32 = jnp.float32
BF16 = jnp.bfloat16
NT = (((1,), (1,)), ((), ()))
TN = (((0,), (0,)), ((), ()))


def exact(a, b, dims):
    return lax.dot_general(a, b, dims, precision=lax.Precision.HIGHEST, preferred_element_type=F32)


def solve_small(matrix, rhs):
    left = 0.5 * (matrix + matrix.T)
    right = rhs
    size = left.shape[0]
    row_at = lax.broadcasted_iota(jnp.int32, left.shape, 0)
    for k in range(size):
        here = row_at == k
        inv = 1.0 / left[k : k + 1, k : k + 1]
        lrow = left[k : k + 1, :] * inv
        rrow = right[k : k + 1, :] * inv
        col = left[:, k : k + 1]
        left = jnp.where(here, lrow, left - col * lrow)
        right = jnp.where(here, rrow, right - col * rrow)
    return right


def kernel(nh, nd, f_hbm, codes_ref, t_ref, g_ref, sol_ref, res_ref,
           fv, rs_send, rs_recv, own, rows0, gr_send, gr_recv, ag, pg_send, pg_recv,
           acc, dr_send, dr_recv, dg_send, dg_recv, dq, d_ref,
           f_sem, rs_ss, rs_rs, gr_ss, gr_rs, ag_ss, ag_rs, pg_ss, pg_rs,
           dr_ss, dr_rs, dg_ss, dg_rs, dq_ss, dq_rs):
    me = lax.axis_index("hidden")
    md = lax.axis_index("dp")
    tokens, width = fv.shape
    seg = tokens // nh
    part = width // nd

    def at_step(i):
        return ((i + nh // 2 - 1) % (nh - 1) + 1) * (1 - i // (nh - 1))

    def rows_of(index):
        return pl.ds(pl.multiple_of(index * seg, seg), seg)

    def f_copy(i):
        t = rows_of((me + at_step(i)) % nh)
        return pltpu.make_async_copy(f_hbm.at[t], fv.at[t], f_sem.at[i])

    def to_hidden(src, dst, ss, rs, d):
        return pltpu.make_async_remote_copy(
            src_ref=src, dst_ref=dst, send_sem=ss.at[d], recv_sem=rs.at[d],
            device_id={"hidden": (me + d) % nh}, device_id_type=pl.DeviceIdType.MESH)

    def to_dp(src, dst, ss, rs, e):
        return pltpu.make_async_remote_copy(
            src_ref=src, dst_ref=dst, send_sem=ss.at[e], recv_sem=rs.at[e],
            device_id={"dp": (md + e) % nd}, device_id_type=pl.DeviceIdType.MESH)

    rs_copy = lambda d: to_hidden(rs_send.at[d], rs_recv.at[d], rs_ss, rs_rs, d)
    gr_copy = lambda d: to_hidden(gr_send, gr_recv.at[d], gr_ss, gr_rs, d)

    nz = 4 if nh % 4 == 0 else 1
    ny = nh // nz

    def ag_copy(s):
        dz, dy = s // ny, s % ny
        handed = (dy + ny - 1) // ny
        to = (me // ny + dz * (1 - handed)) % nz * ny + (me % ny + dy) % ny
        return pltpu.make_async_remote_copy(
            src_ref=ag.at[dz * ny * handed], dst_ref=ag.at[s], send_sem=ag_ss.at[s], recv_sem=ag_rs.at[s],
            device_id={"hidden": to}, device_id_type=pl.DeviceIdType.MESH)

    pg_copy = lambda d: to_hidden(pg_send, pg_recv.at[d], pg_ss, pg_rs, d)
    dr_copy = lambda e: to_dp(dr_send.at[e], dr_recv.at[e], dr_ss, dr_rs, e)
    dg_copy = lambda k, e: to_dp(dg_send, dg_recv.at[k - 1, e], dg_ss.at[k - 1], dg_rs.at[k - 1], e)
    dq_send = lambda e: to_dp(dq.at[md], dq.at[md], dq_ss, dq_rs, e)
    dq_got = lambda e: to_dp(dq.at[md], dq.at[(md + nd - e) % nd], dq_ss, dq_rs, e)

    def each(start, stop, fn):
        def body(i, _):
            fn(i)
            return 0
        lax.fori_loop(start, stop, body, 0)

    each(0, nh, lambda i: f_copy(i).start())

    barrier = pltpu.get_barrier_semaphore()
    each(1, nh, lambda d: pl.semaphore_signal(
        barrier, inc=1, device_id={"hidden": (me + d) % nh}, device_id_type=pl.DeviceIdType.MESH))
    each(1, nd, lambda e: pl.semaphore_signal(
        barrier, inc=1, device_id={"dp": (md + e) % nd}, device_id_type=pl.DeviceIdType.MESH))
    pl.semaphore_wait(barrier, nh - 1 + nd - 1)

    weights = codes_ref[me].astype(F32) * code_scale

    norms = None
    for k in range(ITERS + 1):
        source = g_ref if k == 0 else res_ref
        vec = source[...].astype(BF16)
        if k > 0:
            gr_send[...] = exact(source[...], source[...], NT)
            each(1, nh, lambda d: gr_copy(d).start())

        def forward(i):
            d = at_step(i)
            if k == 0:
                f_copy(i).wait()
            r = lax.dot_general(vec, fv[rows_of((me + d) % nh), :], NT, preferred_element_type=F32)
            own[...] = r
            rs_send[d] = r.astype(BF16)

            @pl.when(i < nh - 1)
            def _():
                rs_copy(d).start()

        each(0, nh, forward)

        if k > 0:
            each(1, nh, lambda d: gr_copy(d).wait())
            fresh = gr_send[...]
            for d in range(1, nh):
                fresh = fresh + gr_recv[d]
            if k > 1:
                mix = solve_small(norms, fresh)
                d_ref[...] = res_ref[...] + exact(mix, d_ref[...], TN)
            norms = fresh

        each(1, nh, lambda i: rs_copy(i).wait())
        rows = own[...]
        for d in range(1, nh):
            rows = rows + rs_recv[d].astype(F32)
        if k > 1:
            rows = rows + exact(mix, rows0[...], TN)
        if 0 < k < ITERS:
            rows0[...] = rows
        scaled = (rows * weights).astype(BF16)
        ag[0] = scaled
        each(0, nz - 1, lambda i: ag_copy(((i + nz // 2 - 1) % (nz - 1) + 1) * ny).start())
        each(1, ny, lambda s: ag_copy(s).start())
        if k > 0:
            local = gr_send[...] if k == 1 else exact(d_ref[...], d_ref[...], NT)
            pg_send[...] = exact(rows, scaled.astype(F32), NT) + (damping / nd) * local
            each(1, nh, lambda d: pg_copy(d).start())

        def came_from(s):
            return (me // ny + nz - s // ny) % nz * ny + (me % ny + ny - s % ny) % ny

        def add_back(s, first):
            seg_rows = rows_of(came_from(s))
            piece = ag[s]
            for c in range(nd):
                got = jnp.dot(piece, fv[seg_rows, c * part : (c + 1) * part], preferred_element_type=F32)
                acc[c] = got if first else acc[c] + got

        add_back(0, True)

        def passing(i):
            s = ((i + nz // 2 - 1) % (nz - 1) + 1) * ny
            ag_copy(s).wait()
            each(1, ny, lambda dy: ag_copy(s + dy).start())
            add_back(s, False)

        def ending(i):
            s = i // (ny - 1) * ny + i % (ny - 1) + 1
            ag_copy(s).wait()
            add_back(s, False)

        each(0, nz - 1, passing)
        each(0, nz * (ny - 1) - 2, ending)
        last = [nh - 3 if ny == 2 else nh - 2, nh - 1]
        for s in last:
            ag_copy(s).wait()

        def final(e):
            c = (md + e) % nd
            columns = pl.ds(pl.multiple_of(c * part, part), part)
            got = acc[c]
            for s in last:
                got = got + jnp.dot(ag[s], fv[rows_of(came_from(s)), columns], preferred_element_type=F32)
            return got

        def finish(i):
            dr_send[i] = final(i).astype(BF16)
            dr_copy(i).start()

        each(1, nd, finish)
        total = final(0)
        if k > 0:
            each(1, nh, lambda d: pg_copy(d).wait())
            dg = pg_send[...]
            for d in range(1, nh):
                dg = dg + pg_recv[d]
            dg_send[...] = dg
            each(1, nd, lambda e: dg_copy(k, e).start())
        each(1, nd, lambda e: dr_copy(e).wait())
        for e in range(1, nd):
            total = total + dr_recv[e].astype(F32)
        dq[md] = total
        each(1, nd, lambda e: dq_send(e).start())
        if k > 0:
            each(1, nd, lambda e: dg_copy(k, e).wait())
            curv = dg_send[...]
            for e in range(1, nd):
                curv = curv + dg_recv[k - 1, e]
            step_mix = solve_small(curv, norms)
        each(1, nd, lambda e: dq_got(e).wait())
        applied = jnp.concatenate([dq[c] for c in range(nd)], axis=1)
        if k == 0:
            residual = t_ref[...] - (applied + damping * g_ref[...])
            res_ref[...] = residual
            d_ref[...] = residual
        else:
            applied = applied + damping * d_ref[...]
            before = g_ref[...] if k == 1 else sol_ref[...]
            sol_ref[...] = before + exact(step_mix, d_ref[...], TN)
            res_ref[...] = res_ref[...] - exact(step_mix, applied, TN)


def shards(nh, nd, features, codes, targets, guess):
    tokens, width = features.shape
    rhs = guess.shape[1]
    seg = tokens // nh
    part = width // nd
    vmem = pl.BlockSpec(memory_space=pltpu.VMEM)
    flat = jax.ShapeDtypeStruct((rhs, width), F32)
    dma = pltpu.SemaphoreType.DMA
    sol, res = pl.pallas_call(
        functools.partial(kernel, nh, nd),
        out_shape=(flat, flat),
        in_specs=[pl.BlockSpec(memory_space=pl.ANY), vmem, vmem, vmem],
        out_specs=(vmem, vmem),
        scratch_shapes=[
            pltpu.VMEM((tokens, width), BF16),
            pltpu.VMEM((nh, rhs, seg), BF16),
            pltpu.VMEM((nh, rhs, seg), BF16),
            pltpu.VMEM((rhs, seg), F32),
            pltpu.VMEM((rhs, seg), F32),
            pltpu.VMEM((rhs, rhs), F32),
            pltpu.VMEM((nh, rhs, rhs), F32),
            pltpu.VMEM((nh, rhs, seg), BF16),
            pltpu.VMEM((rhs, rhs), F32),
            pltpu.VMEM((nh, rhs, rhs), F32),
            pltpu.VMEM((nd, rhs, part), F32),
            pltpu.VMEM((nd, rhs, part), BF16),
            pltpu.VMEM((nd, rhs, part), BF16),
            pltpu.VMEM((rhs, rhs), F32),
            pltpu.VMEM((ITERS, nd, rhs, rhs), F32),
            pltpu.VMEM((nd, rhs, part), F32),
            pltpu.VMEM((rhs, width), F32),
            dma((nh,)),
            dma((nh,)), dma((nh,)), dma((nh,)), dma((nh,)),
            dma((nh,)), dma((nh,)), dma((nh,)), dma((nh,)),
            dma((nd,)), dma((nd,)), dma((ITERS, nd)), dma((ITERS, nd)), dma((nd,)), dma((nd,)),
        ],
        compiler_params=pltpu.CompilerParams(
            collective_id=0, has_side_effects=True, vmem_limit_bytes=56 * 1024 * 1024),
        cost_estimate=pl.CostEstimate(
            flops=12 * tokens * width * rhs, bytes_accessed=2 * tokens * width, transcendentals=0),
    )(features, codes.reshape(nh, 1, seg), targets.T, guess.T)
    return sol.T, res.T


def solution(mesh):
    nh, nd = mesh.shape["hidden"], mesh.shape["dp"]
    in_specs = (P("dp", "hidden"), P("dp"), P("hidden", None), P("hidden", None))
    out_specs = (P("hidden", None), P("hidden", None))
    return jax.shard_map(functools.partial(shards, nh, nd), mesh=mesh, in_specs=in_specs,
                         out_specs=out_specs, check_vma=False)
```

```python
import functools

import jax
import jax.numpy as jnp
from jax import lax
from jax.experimental import pallas as pl
from jax.experimental.pallas import tpu as pltpu
from jax.sharding import PartitionSpec as P

ITERS = 2
damping = 0.5
code_scale = 0.25

F32 = jnp.float32
BF16 = jnp.bfloat16
NT = (((1,), (1,)), ((), ()))
TN = (((0,), (0,)), ((), ()))


def exact(a, b, dims):
    return lax.dot_general(a, b, dims, precision=lax.Precision.HIGHEST, preferred_element_type=F32)


def solve_small(matrix, rhs):
    left = 0.5 * (matrix + matrix.T)
    right = rhs
    size = left.shape[0]
    row_at = lax.broadcasted_iota(jnp.int32, left.shape, 0)
    for k in range(size):
        here = row_at == k
        inv = 1.0 / left[k : k + 1, k : k + 1]
        lrow = left[k : k + 1, :] * inv
        rrow = right[k : k + 1, :] * inv
        col = left[:, k : k + 1]
        left = jnp.where(here, lrow, left - col * lrow)
        right = jnp.where(here, rrow, right - col * rrow)
    return right


def kernel(nh, nd, f_hbm, codes_ref, t_ref, g_ref, sol_ref, res_ref,
           fv, rs_send, rs_recv, own, rows0, gr_send, gr_recv, ag, pg_send, pg_recv,
           acc, dr_send, dr_recv, dg_send, dg_recv, dq, d_ref,
           f_sem, rs_ss, rs_rs, gr_ss, gr_rs, ag_ss, ag_rs, pg_ss, pg_rs,
           dr_ss, dr_rs, dg_ss, dg_rs, dq_ss, dq_rs):
    me = lax.axis_index("hidden")
    md = lax.axis_index("dp")
    tokens, width = fv.shape
    seg = tokens // nh
    part = width // nd

    def at_step(i):
        return ((i + nh // 2 - 1) % (nh - 1) + 1) * (1 - i // (nh - 1))

    def rows_of(index):
        return pl.ds(pl.multiple_of(index * seg, seg), seg)

    def f_copy(i):
        t = rows_of((me + at_step(i)) % nh)
        return pltpu.make_async_copy(f_hbm.at[t], fv.at[t], f_sem.at[i])

    def to_hidden(src, dst, ss, rs, d):
        return pltpu.make_async_remote_copy(
            src_ref=src, dst_ref=dst, send_sem=ss.at[d], recv_sem=rs.at[d],
            device_id={"hidden": (me + d) % nh}, device_id_type=pl.DeviceIdType.MESH)

    def to_dp(src, dst, ss, rs, e):
        return pltpu.make_async_remote_copy(
            src_ref=src, dst_ref=dst, send_sem=ss.at[e], recv_sem=rs.at[e],
            device_id={"dp": (md + e) % nd}, device_id_type=pl.DeviceIdType.MESH)

    rs_copy = lambda d: to_hidden(rs_send.at[d], rs_recv.at[d], rs_ss, rs_rs, d)
    gr_copy = lambda d: to_hidden(gr_send, gr_recv.at[d], gr_ss, gr_rs, d)

    nz = 4 if nh % 4 == 0 else 1
    ny = nh // nz

    def ag_copy(s):
        dz, dy = s // ny, s % ny
        handed = (dy + ny - 1) // ny
        to = (me // ny + dz * (1 - handed)) % nz * ny + (me % ny + dy) % ny
        return pltpu.make_async_remote_copy(
            src_ref=ag.at[dz * ny * handed], dst_ref=ag.at[s], send_sem=ag_ss.at[s], recv_sem=ag_rs.at[s],
            device_id={"hidden": to}, device_id_type=pl.DeviceIdType.MESH)

    pg_copy = lambda d: to_hidden(pg_send, pg_recv.at[d], pg_ss, pg_rs, d)
    dr_copy = lambda e: to_dp(dr_send.at[e], dr_recv.at[e], dr_ss, dr_rs, e)
    dg_copy = lambda k, e: to_dp(dg_send, dg_recv.at[k - 1, e], dg_ss.at[k - 1], dg_rs.at[k - 1], e)
    dq_send = lambda e: to_dp(dq.at[md], dq.at[md], dq_ss, dq_rs, e)
    dq_got = lambda e: to_dp(dq.at[md], dq.at[(md + nd - e) % nd], dq_ss, dq_rs, e)

    def each(start, stop, fn):
        def body(i, _):
            fn(i)
            return 0
        lax.fori_loop(start, stop, body, 0)

    each(0, nh, lambda i: f_copy(i).start())

    barrier = pltpu.get_barrier_semaphore()
    each(1, nh, lambda d: pl.semaphore_signal(
        barrier, inc=1, device_id={"hidden": (me + d) % nh}, device_id_type=pl.DeviceIdType.MESH))
    each(1, nd, lambda e: pl.semaphore_signal(
        barrier, inc=1, device_id={"dp": (md + e) % nd}, device_id_type=pl.DeviceIdType.MESH))
    pl.semaphore_wait(barrier, nh - 1 + nd - 1)

    weights = codes_ref[me].astype(F32) * code_scale

    norms = None
    for k in range(ITERS + 1):
        source = g_ref if k == 0 else res_ref
        vec = source[...].astype(BF16)
        if k > 0:
            gr_send[...] = exact(source[...], source[...], NT)
            each(1, nh, lambda d: gr_copy(d).start())

        def forward(i):
            d = at_step(i)
            if k == 0:
                f_copy(i).wait()
            r = lax.dot_general(vec, fv[rows_of((me + d) % nh), :], NT, preferred_element_type=F32)
            own[...] = r
            rs_send[d] = r.astype(BF16)

            @pl.when(i < nh - 1)
            def _():
                rs_copy(d).start()

        each(0, nh, forward)

        if k > 0:
            each(1, nh, lambda d: gr_copy(d).wait())
            fresh = gr_send[...]
            for d in range(1, nh):
                fresh = fresh + gr_recv[d]
            if k > 1:
                mix = solve_small(norms, fresh)
                d_ref[...] = res_ref[...] + exact(mix, d_ref[...], TN)
            norms = fresh

        each(1, nh, lambda i: rs_copy(i).wait())
        rows = own[...]
        for d in range(1, nh):
            rows = rows + rs_recv[d].astype(F32)
        if k > 1:
            rows = rows + exact(mix, rows0[...], TN)
        if 0 < k < ITERS:
            rows0[...] = rows
        scaled = (rows * weights).astype(BF16)
        ag[0] = scaled
        each(0, nz - 1, lambda i: ag_copy(((i + nz // 2 - 1) % (nz - 1) + 1) * ny).start())
        each(1, ny, lambda s: ag_copy(s).start())
        if k > 0:
            local = gr_send[...] if k == 1 else exact(d_ref[...], d_ref[...], NT)
            pg_send[...] = exact(rows, scaled.astype(F32), NT) + (damping / nd) * local
            each(1, nh, lambda d: pg_copy(d).start())

        def came_from(s):
            return (me // ny + nz - s // ny) % nz * ny + (me % ny + ny - s % ny) % ny

        def add_back(s, first):
            seg_rows = rows_of(came_from(s))
            piece = ag[s]
            for c in range(nd):
                got = jnp.dot(piece, fv[seg_rows, c * part : (c + 1) * part], preferred_element_type=F32)
                acc[c] = got if first else acc[c] + got

        add_back(0, True)

        def passing(i):
            s = ((i + nz // 2 - 1) % (nz - 1) + 1) * ny
            ag_copy(s).wait()
            each(1, ny, lambda dy: ag_copy(s + dy).start())
            add_back(s, False)

        def ending(i):
            s = i // (ny - 1) * ny + i % (ny - 1) + 1
            ag_copy(s).wait()
            add_back(s, False)

        each(0, nz - 1, passing)
        each(0, nz * (ny - 1) - 2, ending)
        last = [nh - 3, nh - 1] if ny == 2 else [nh - 2, nh - 1]
        for s in last:
            ag_copy(s).wait()

        def final(e):
            c = (md + e) % nd
            columns = pl.ds(pl.multiple_of(c * part, part), part)
            got = acc[c]
            for s in last:
                got = got + jnp.dot(ag[s], fv[rows_of(came_from(s)), columns], preferred_element_type=F32)
            return got

        def finish(i):
            dr_send[i] = final(i).astype(BF16)
            dr_copy(i).start()

        each(1, nd, finish)
        total = final(0)
        if k > 0:
            each(1, nh, lambda d: pg_copy(d).wait())
            dg = pg_send[...]
            for d in range(1, nh):
                dg = dg + pg_recv[d]
            dg_send[...] = dg
            each(1, nd, lambda e: dg_copy(k, e).start())
        each(1, nd, lambda e: dr_copy(e).wait())
        for e in range(1, nd):
            total = total + dr_recv[e].astype(F32)
        dq[md] = total.astype(BF16)
        each(1, nd, lambda e: dq_send(e).start())
        if k > 0:
            each(1, nd, lambda e: dg_copy(k, e).wait())
            curv = dg_send[...]
            for e in range(1, nd):
                curv = curv + dg_recv[k - 1, e]
            step_mix = solve_small(curv, norms)
        each(1, nd, lambda e: dq_got(e).wait())
        applied = jnp.concatenate([dq[c].astype(F32) for c in range(nd)], axis=1)
        if k == 0:
            residual = t_ref[...] - (applied + damping * g_ref[...])
            res_ref[...] = residual
            d_ref[...] = residual
        else:
            applied = applied + damping * d_ref[...]
            before = g_ref[...] if k == 1 else sol_ref[...]
            sol_ref[...] = before + exact(step_mix, d_ref[...], TN)
            res_ref[...] = res_ref[...] - exact(step_mix, applied, TN)


def shards(nh, nd, features, codes, targets, guess):
    tokens, width = features.shape
    rhs = guess.shape[1]
    seg = tokens // nh
    part = width // nd
    vmem = pl.BlockSpec(memory_space=pltpu.VMEM)
    flat = jax.ShapeDtypeStruct((rhs, width), F32)
    dma = pltpu.SemaphoreType.DMA
    sol, res = pl.pallas_call(
        functools.partial(kernel, nh, nd),
        out_shape=(flat, flat),
        in_specs=[pl.BlockSpec(memory_space=pl.ANY), vmem, vmem, vmem],
        out_specs=(vmem, vmem),
        scratch_shapes=[
            pltpu.VMEM((tokens, width), BF16),
            pltpu.VMEM((nh, rhs, seg), BF16),
            pltpu.VMEM((nh, rhs, seg), BF16),
            pltpu.VMEM((rhs, seg), F32),
            pltpu.VMEM((rhs, seg), F32),
            pltpu.VMEM((rhs, rhs), F32),
            pltpu.VMEM((nh, rhs, rhs), F32),
            pltpu.VMEM((nh, rhs, seg), BF16),
            pltpu.VMEM((rhs, rhs), F32),
            pltpu.VMEM((nh, rhs, rhs), F32),
            pltpu.VMEM((nd, rhs, part), F32),
            pltpu.VMEM((nd, rhs, part), BF16),
            pltpu.VMEM((nd, rhs, part), BF16),
            pltpu.VMEM((rhs, rhs), F32),
            pltpu.VMEM((ITERS, nd, rhs, rhs), F32),
            pltpu.VMEM((nd, rhs, part), BF16),
            pltpu.VMEM((rhs, width), F32),
            dma((nh,)),
            dma((nh,)), dma((nh,)), dma((nh,)), dma((nh,)),
            dma((nh,)), dma((nh,)), dma((nh,)), dma((nh,)),
            dma((nd,)), dma((nd,)), dma((ITERS, nd)), dma((ITERS, nd)), dma((nd,)), dma((nd,)),
        ],
        compiler_params=pltpu.CompilerParams(
            collective_id=0, has_side_effects=True, vmem_limit_bytes=56 * 1024 * 1024),
        cost_estimate=pl.CostEstimate(
            flops=12 * tokens * width * rhs, bytes_accessed=2 * tokens * width, transcendentals=0),
    )(features, codes.reshape(nh, 1, seg), targets.T, guess.T)
    return sol.T, res.T


def solution(mesh):
    nh, nd = mesh.shape["hidden"], mesh.shape["dp"]
    in_specs = (P("dp", "hidden"), P("dp"), P("hidden", None), P("hidden", None))
    out_specs = (P("hidden", None), P("hidden", None))
    return jax.shard_map(functools.partial(shards, nh, nd), mesh=mesh, in_specs=in_specs,
                         out_specs=out_specs, check_vma=False)
```
